512 devices in a mesh: gx: 32 (over z, x_hi), gy: 16 (over y, x_lo, core).
Axes of the slice: x: 4 (x_hi: 2, x_lo: 2; x = x_hi * 2 + x_lo), y: 4, z: 16, core: 2. Of those that a mesh axis runs over, the one named last changes fastest.
Arguments:
- flow_field: bfloat16 [1024, 512, 2048], P('gx', 'gy'), may hold values from -6 to 6
- y_factor: bfloat16 [512, 128], P('gy'), may hold values from -0.25 to 0.25
- z_factor: bfloat16 [64, 16], replicated, may hold values from -0.75 to 0.75
- v_factor: bfloat16 [32, 8], replicated, may hold values from -1 to 1
- x_start: float32 [1024, 128], P('gx'), may hold values from -0.1875 to 0.1875
Outputs:
- x_factor: float32 [1024, 128], P('gx')
- core_tensor: float32 [128, 16384], P('gx', 'gy')
The draws below stay inside these ranges and needn't reach their ends.
All inputs are finite; a program needn't handle non-finite values.
Results may differ from the reference program's by a relative error of at most 0.0051.
Values sent between devices are 32-bit elements; how exact they have to be, the bound alone decides.
No kernel may reach another device: no remote copies, remote signals or barrier semaphores. Data moves between devices by JAX's collectives and lax.ppermute only.
A program may use at most 64 MiB of HBM per device.

```python
import jax
import jax.numpy as jnp
from jax import lax

NZ = 64
NV = 32
RX = 128
RY = 128
RZ = 16
RV = 8
ITERS = 3
NX = 1024
NY = 512


def block_scale(rng, dims, split, smallest, largest):
    def one(position, blocks):
        heights = jax.random.uniform(jax.random.fold_in(jax.random.fold_in(rng, 6), position), (blocks,), jnp.float32, smallest / len(split), largest / len(split))
        return jnp.repeat(jnp.exp(heights), dims[position] // blocks).reshape((-1,) + (1,) * (len(dims) - position - 1))

    factor_of = one(*split[0])
    for cut in split[1:]:
        factor_of = factor_of * one(*cut)
    return factor_of


def gaussian(key, dims, scale, most, pieces=(), dtype=jnp.bfloat16):
    loudness = block_scale(key, dims, pieces, -0.22, 0.18) if pieces else 1.0
    entries = jax.random.normal(key, dims, jnp.float32) * scale * loudness
    return jnp.minimum(jnp.maximum(entries, -most), most).astype(dtype)


def setup_inputs(seed: int = 0) -> dict:
    streams_of = jax.random.split(jax.random.key(seed), 6)
    flow_field = gaussian(streams_of[0], (NX, NY, NZ * NV), 1.0, 6.0, ((0, 32), (1, 16)))
    y_factor = gaussian(streams_of[1], (NY, RY), NY ** -0.5, 0.25, ((0, 16),))
    z_factor = gaussian(streams_of[2], (NZ, RZ), NZ ** -0.5, 0.75)
    v_factor = gaussian(streams_of[3], (NV, RV), NV ** -0.5, 1.0)
    x_start = gaussian(streams_of[4], (NX, RX), NX ** -0.5, 0.1875, ((0, 32),), jnp.float32)
    return {"flow_field": flow_field, "y_factor": y_factor, "z_factor": z_factor, "v_factor": v_factor, "x_start": x_start}


def kronecker_table(z_factor, v_factor):
    table = z_factor.astype(jnp.float32)[:, None, :, None] * v_factor.astype(jnp.float32)[None, :, None, :]
    return table.reshape(NZ * NV, RZ * RV).astype(jnp.bfloat16)

def orthonormal(image_rows):
    correlation = jnp.dot(image_rows.T, image_rows, precision=lax.Precision.HIGHEST)
    lower_factor = jnp.linalg.cholesky(correlation)
    return lax.linalg.triangular_solve(lower_factor, image_rows, left_side=False, lower=True, transpose_a=True)

def reference(flow_field, y_factor, z_factor, v_factor, x_start):
    kronecker = kronecker_table(z_factor, v_factor)
    reduced = jnp.dot(flow_field.reshape(NX * NY, NZ * NV).astype(jnp.float32), kronecker.astype(jnp.float32), preferred_element_type=jnp.float32)
    reduced = reduced.astype(jnp.bfloat16).reshape(NX, NY, RZ * RV)
    projected = jnp.einsum('ayk,yq->aqk', reduced.astype(jnp.float32), y_factor.astype(jnp.float32))
    projected = projected.reshape(NX, RY * RZ * RV)
    basis_now = x_start
    for sweep in range(ITERS):
        left_side = jnp.dot(projected.T, basis_now, precision=lax.Precision.HIGHEST)
        image_rows = jnp.dot(projected, left_side, precision=lax.Precision.HIGHEST)
        basis_now = orthonormal(image_rows)
    core_tensor = jnp.dot(basis_now.T, projected, precision=lax.Precision.HIGHEST)
    return (basis_now, core_tensor)
```

```python
import jax
import jax.numpy as jnp
from jax import lax
from jax.sharding import Mesh, PartitionSpec as P

NZ = 64
NV = 32
RX = 128
RY = 128
RZ = 16
RV = 8
ITERS = 3
HIGHEST = lax.Precision.HIGHEST
PLANE = ("h", "y", "l", "c")
XY = ("h", "y", "l")


def kronecker_table(z_factor, v_factor):
    table = (
        z_factor.astype(jnp.float32)[:, None, :, None]
        * v_factor.astype(jnp.float32)[None, :, None, :]
    )
    return table.reshape(NZ * NV, RZ * RV).astype(jnp.bfloat16)


def gather_by_exchange(block, axes):
    count = lax.axis_size(axes)
    return lax.all_to_all(jnp.broadcast_to(block[None], (count, *block.shape)), axes, 0, 0)


def orthonormal(image_rows):
    correlation = lax.dot_general(
        image_rows, image_rows, (((0,), (0,)), ((), ())), precision=HIGHEST
    )
    lower_factor = jnp.linalg.cholesky(correlation)
    return lax.linalg.triangular_solve(
        lower_factor, image_rows, left_side=False, lower=True, transpose_a=True
    )


def local(flow_field, y_factor, z_factor, v_factor, x_start):
    z = lax.axis_index("z")
    h = lax.axis_index("h")
    kronecker = kronecker_table(z_factor, v_factor)
    reduced = lax.dot_general(
        kronecker,
        flow_field.reshape(1024, NZ * NV),
        (((0,), (1,)), ((), ())),
        preferred_element_type=jnp.float32,
    )
    reduced = lax.reduce_precision(reduced, 8, 7)
    y_half = lax.dynamic_slice_in_dim(y_factor, h * 16, 16, 0).astype(jnp.float32)
    send = jnp.concatenate(
        [reduced.reshape(32, 32, 128), jnp.broadcast_to(y_half[None], (32, 16, 128))], axis=1
    )
    got = lax.all_to_all(send, PLANE, 0, 0).reshape(2, 16, 48, 128)
    table = got[:, :, 32:, :].transpose(1, 0, 2, 3).reshape(16, 32, 128)
    rows = got[:, :, :32, :].reshape(2, 16, 4, 8, 4, 32)
    projected = jnp.einsum(
        "hgkjay,gyq->hjakq", rows, table, precision=HIGHEST
    ).reshape(64, 512)
    start = gather_by_exchange(x_start, "h").reshape(64, RX)
    basis = lax.all_gather(start, "z").reshape(1024, RX)
    every = lax.all_gather(projected, "z").reshape(1024, 512)
    gram = lax.dot_general(every, every, (((1,), (1,)), ((), ())), precision=HIGHEST)
    gram = lax.all_to_all(gram.reshape(2, 512, 1024), "c", 0, 0).sum(0)
    gram = lax.all_to_all(gram.reshape(16, 32, 1024), XY, 0, 0).sum(0)
    gram = gather_by_exchange(gram, XY).reshape(512, 1024)
    gram = gather_by_exchange(gram, "c").reshape(1024, 1024)
    for sweep in range(ITERS):
        basis = orthonormal(jnp.dot(gram, basis, precision=HIGHEST))
    x_factor = lax.dynamic_slice_in_dim(basis, (z * 2 + h) * 32, 32, 0)
    mine = lax.dynamic_slice_in_dim(basis, z * 8, 8, 1)
    core = lax.dot_general(mine, every, (((0,), (0,)), ((), ())), precision=HIGHEST)
    core = core.reshape(2, 4, 4, 16, 8).transpose(0, 3, 1, 2, 4).reshape(32, 1, 128)
    core = lax.all_to_all(core, PLANE, 0, 0).reshape(32, 4, 4, 8)
    core = core.transpose(1, 3, 0, 2).reshape(4, 1024)
    return (x_factor, core)


def solution(mesh):
    fine = Mesh(mesh.devices.reshape(16, 2, 4, 2, 2), ("z", "h", "y", "l", "c"))
    gx, gy = ("z", "h"), ("y", "l", "c")
    placed = (P(gx, gy, None), P(gy, None), P(), P(), P(gx, None))
    return jax.shard_map(
        local, mesh=fine, in_specs=placed, out_specs=(P(gx, None), P(gx, gy)), check_vma=False
    )
```

```python
import jax
import jax.numpy as jnp
from jax import lax
from jax.experimental import pallas as pl
from jax.experimental.pallas import tpu as pltpu
from jax.sharding import Mesh, PartitionSpec as P

NZ = 64
NV = 32
RX = 128
RY = 128
RZ = 16
RV = 8
ITERS = 3
HIGHEST = lax.Precision.HIGHEST
PLANE = ("h", "y", "l", "c")
XY = ("h", "y", "l")
PART = 168
NN = (((1,), (0,)), ((), ()))
NT = (((1,), (1,)), ((), ()))


def dot(a, b, dims):
    return lax.dot_general(a, b, dims, precision=HIGHEST, preferred_element_type=jnp.float32)


def kronecker_table(z_factor, v_factor):
    table = (
        z_factor.astype(jnp.float32)[:, None, :, None]
        * v_factor.astype(jnp.float32)[None, :, None, :]
    )
    return table.reshape(NZ * NV, RZ * RV).astype(jnp.bfloat16)


def strips_kernel(where_ref, *refs):
    blocks, out_ref = refs[:9], refs[9]
    odd = lax.rem(where_ref[0], 2)
    for t in range(4):
        near = blocks[4 + t][...]
        if t == 0:
            near = near * 0.5
        far = blocks[5 + t][...]
        swap = odd != (t % 2)
        pair = jnp.concatenate([jnp.where(swap, far, near), jnp.where(swap, near, far)], axis=0)
        tile = dot(blocks[4 - t][...], pair, NT)
        for g in range(8):
            out_ref[t * 8 + g, 0:8, :] = tile[8 * g : 8 * g + 8, :]
    last = dot(blocks[0][...], blocks[8][...], NT)
    last = jnp.concatenate([last[:32, :], last[32:, :]], axis=1)
    for p in range(32):
        out_ref[p, 8:16, :] = jnp.broadcast_to(last[p : p + 1, :], (8, 128))


def strips(z, blocks):
    return pl.pallas_call(
        strips_kernel,
        out_shape=jax.ShapeDtypeStruct((32, 16, 128), jnp.float32),
        in_specs=[pl.BlockSpec(memory_space=pltpu.SMEM)]
        + [pl.BlockSpec(memory_space=pltpu.VMEM)] * 9,
        out_specs=pl.BlockSpec(memory_space=pltpu.VMEM),
        compiler_params=pltpu.CompilerParams(vmem_limit_bytes=24 * 1024 * 1024),
        name="strips",
    )(z.reshape(1), *blocks)


def inverse_lower(correlation):
    full = (8, 128)
    sub = lax.broadcasted_iota(jnp.int32, full, 0)
    lane = lax.broadcasted_iota(jnp.int32, full, 1)
    left = [correlation[8 * v : 8 * v + 8, :] for v in range(16)]
    right = [jnp.where(lane == sub + 8 * v, 1.0, 0.0) for v in range(16)]
    done = []

    def row(x, i):
        return jnp.broadcast_to(x[i : i + 1, :], full)

    def column(x, j):
        return jnp.broadcast_to(x[:, j : j + 1], full)

    for v in range(16):
        small = [column(left[v], 8 * v + i) for i in range(8)]
        rest, made = left[v], right[v]
        finished = jnp.zeros(full, jnp.float32)
        for i in range(8):
            pivot = row(small[i], i)
            inverse = 1.0 / pivot
            here = sub == i
            share = jnp.where(here, -inverse, small[i] * inverse)
            made_row = row(made, i)
            root = lax.rsqrt(pivot)
            root = root * (1.5 - 0.5 * pivot * root * root)
            finished = jnp.where(here, made_row * root, finished)
            made = jnp.where(here, 0.0, made) - share * made_row
            if v < 15:
                rest = jnp.where(here, 0.0, rest) - share * row(rest, i)
            for k in range(i + 1, 8):
                small[k] = jnp.where(here, 0.0, small[k]) - share * row(small[k], i)
        done.append(finished)
        if v < 15:
            rest_rows = [row(rest, i) for i in range(8)]
            made_rows = [row(made, i) for i in range(8)]
            for w in range(v + 1, 16):
                shares = [column(left[w], 8 * v + i) for i in range(8)]
                taken = [shares[i] * rest_rows[i] for i in range(8)]
                left[w] = left[w] - (
                    ((taken[0] + taken[1]) + (taken[2] + taken[3]))
                    + ((taken[4] + taken[5]) + (taken[6] + taken[7]))
                )
                taken = [shares[i] * made_rows[i] for i in range(8)]
                right[w] = right[w] - (
                    ((taken[0] + taken[1]) + (taken[2] + taken[3]))
                    + ((taken[4] + taken[5]) + (taken[6] + taken[7]))
                )
    return jnp.concatenate(done, axis=0)


def sweeps_kernel(where_ref, mine, other, every, rows_ref, core_ref, parts, half, far, start, basis, sems):
    z, h, c = where_ref[0], where_ref[1], where_ref[2]
    first = pltpu.make_async_copy(mine, parts.at[c], sems.at[0])
    second = pltpu.make_async_copy(other, parts.at[1 - c], sems.at[1])
    first.start()
    second.start()
    first.wait()
    second.wait()
    lower_lanes = lax.broadcasted_iota(jnp.int32, (8, 128), 1) < 64

    for zz in range(16):
        for hh in range(2):
            for cc in range(2):
                for e in range(2):
                    start[pl.ds(zz * 64 + hh * 32 + 2 * cc + e, 8, stride=4), :] = parts[
                        cc, pl.ds(hh * 8 * PART + 136 + 2 * zz + e, 8, stride=PART), :
                    ]
    for zz in range(16):
        basis[:, zz * 64 : zz * 64 + 64] = start[zz * 64 : zz * 64 + 64, :].T

    for zz in range(8):
        for cc in range(2):
            for g in range(2):
                far[pl.ds(zz * 32 + cc + 16 * g, 8, stride=2), :] = parts[
                    cc, pl.ds(g * 8 * PART + 128 + zz, 8, stride=PART), :
                ]

    def source(row_z, col_z, g):
        d = (col_z - row_z) % 16
        z_of = (row_z + d // 2) % 16
        if d < 8:
            p = (d // 2) * 8 + g
            base = (p // 2) * PART + z_of * 8
            return parts[p % 2, base : base + 8, :]
        if d == 8 and z_of < 8:
            block = far[z_of * 32 + (g % 4) * 8 : z_of * 32 + (g % 4) * 8 + 8, :]
            if (g >= 4) != (col_z % 2 == 1):
                block = pltpu.roll(block, 64, 1)
            return block
        return jnp.zeros((8, 128), jnp.float32)

    for row_z in range(16):
        for pair in range(8):
            for g in range(8):
                a = source(row_z, 2 * pair, g)
                b = source(row_z, 2 * pair + 1, g)
                half[row_z * 64 + g * 8 : row_z * 64 + g * 8 + 8, pair * 128 : pair * 128 + 128] = (
                    jnp.where(lower_lanes, a, b)
                )

    def sweep(_, carry):
        now = basis[...]
        image = dot(now, half[...], NN) + dot(now, half[...], NT)
        correlation = dot(image, image, NT)
        basis[...] = dot(inverse_lower(correlation), image, NN)
        return carry

    lax.fori_loop(0, ITERS, sweep, 0)
    pick = lax.broadcasted_iota(jnp.int32, (32, 1024), 1) == (
        lax.broadcasted_iota(jnp.int32, (32, 1024), 0) + (z * 2 + h) * 32
    )
    rows_ref[...] = dot(jnp.where(pick, 1.0, 0.0), basis[...], NT)
    core_ref[...] = dot(basis[pl.ds(pl.multiple_of(z * 8, 8), 8), :], every[...], NN)


def sweeps(where, mine, other, every):
    return pl.pallas_call(
        sweeps_kernel,
        out_shape=(
            jax.ShapeDtypeStruct((32, RX), jnp.float32),
            jax.ShapeDtypeStruct((8, 512), jnp.float32),
        ),
        in_specs=[
            pl.BlockSpec(memory_space=pltpu.SMEM),
            pl.BlockSpec(memory_space=pl.ANY),
            pl.BlockSpec(memory_space=pl.ANY),
            pl.BlockSpec(memory_space=pltpu.VMEM),
        ],
        out_specs=[pl.BlockSpec(memory_space=pltpu.VMEM)] * 2,
        scratch_shapes=[
            pltpu.VMEM((2, 16 * PART, 128), jnp.float32),
            pltpu.VMEM((1024, 1024), jnp.float32),
            pltpu.VMEM((8 * 32, 128), jnp.float32),
            pltpu.VMEM((1024, 128), jnp.float32),
            pltpu.VMEM((128, 1024), jnp.float32),
            pltpu.SemaphoreType.DMA((2,)),
        ],
        compiler_params=pltpu.CompilerParams(vmem_limit_bytes=48 * 1024 * 1024),
        name="sweeps",
    )(where, mine, other, every)


def local(flow_field, y_factor, z_factor, v_factor, x_start):
    z = lax.axis_index("z").astype(jnp.int32)
    h = lax.axis_index("h").astype(jnp.int32)
    c = lax.axis_index("c").astype(jnp.int32)
    kronecker = kronecker_table(z_factor, v_factor)
    reduced = lax.dot_general(
        kronecker,
        flow_field.reshape(1024, NZ * NV),
        (((0,), (1,)), ((), ())),
        preferred_element_type=jnp.float32,
    )
    reduced = lax.reduce_precision(reduced, 8, 7)
    y_half = lax.dynamic_slice_in_dim(y_factor, h * 16, 16, 0).astype(jnp.float32)
    send = jnp.concatenate(
        [reduced.reshape(32, 32, 128), jnp.broadcast_to(y_half[None], (32, 16, 128))], axis=1
    )
    got = lax.all_to_all(send, PLANE, 0, 0).reshape(2, 16, 48, 128)
    table = got[:, :, 32:, :].transpose(1, 0, 2, 3).reshape(16, 32, 128)
    rows = got[:, :, :32, :].reshape(2, 16, 4, 8, 4, 32)
    projected = jnp.einsum("hgkjay,gyq->hjakq", rows, table, precision=HIGHEST).reshape(64, 512)

    below, above = [projected], [projected]
    from_above = [(i, (i - 1) % 16) for i in range(16)]
    from_below = [(i, (i + 1) % 16) for i in range(16)]
    for _ in range(4):
        above.append(lax.ppermute(above[-1], "z", from_above))
        below.append(lax.ppermute(below[-1], "z", from_below))
    blocks = below[:0:-1] + above
    tied, *_ = lax.optimization_barrier((projected, below[-1], above[-1]))
    every = lax.all_gather(tied, "z").reshape(1024, 512)

    part = lax.all_to_all(strips(z, blocks), PLANE, 0, 0).sum(0)
    gy = (lax.axis_index("y") * 4 + lax.axis_index("l") * 2 + c).astype(jnp.int32)
    start = lax.dynamic_slice_in_dim(x_start, 2 * gy, 2, 0)
    part = jnp.concatenate([part[:9], start, jnp.zeros((5, 128), jnp.float32)], axis=0)
    line = lax.all_gather(part, "z")
    line = jnp.concatenate(
        [line[:, :8].reshape(128, 128), line[:8, 8], line[:, 9:11].reshape(32, 128)], axis=0
    )
    mine = lax.all_to_all(jnp.broadcast_to(line[None], (16, PART, 128)), XY, 0, 0)
    mine = mine.reshape(16 * PART, 128)
    other = lax.ppermute(mine, "c", [(0, 1), (1, 0)])

    x_factor, core = sweeps(jnp.stack([z, h, c]), mine, other, every)
    core = core.reshape(2, 4, 4, 16, 8).transpose(0, 3, 1, 2, 4).reshape(32, 1, 128)
    core = lax.all_to_all(core, PLANE, 0, 0).reshape(32, 4, 4, 8)
    core = core.transpose(1, 3, 0, 2).reshape(4, 1024)
    return (x_factor, core)


def solution(mesh):
    fine = Mesh(mesh.devices.reshape(16, 2, 4, 2, 2), ("z", "h", "y", "l", "c"))
    gx, gy = ("z", "h"), ("y", "l", "c")
    placed = (P(gx, gy, None), P(gy, None), P(), P(), P(gx, None))
    return jax.shard_map(
        local, mesh=fine, in_specs=placed, out_specs=(P(gx, None), P(gx, gy)), check_vma=False
    )
```

```python
import jax
import jax.numpy as jnp
from jax import lax
from jax.experimental import pallas as pl
from jax.experimental.pallas import tpu as pltpu
from jax.sharding import Mesh, PartitionSpec as P

NZ = 64
NV = 32
RX = 128
RY = 128
RZ = 16
RV = 8
ITERS = 3
HIGHEST = lax.Precision.HIGHEST
PLANE = ("h", "y", "l", "c")
XY = ("h", "y", "l")
PART = 168
NN = (((1,), (0,)), ((), ()))
NT = (((1,), (1,)), ((), ()))
TN = (((0,), (0,)), ((), ()))
BLOCKS = 4


def dot(a, b, dims):
    return lax.dot_general(a, b, dims, precision=HIGHEST, preferred_element_type=jnp.float32)


def reduced_kernel(where_ref, flow, y_ref, z_ref, v_ref, out_ref, held, table, turned, sems):
    size = 1024 // BLOCKS

    def fetch(j):
        return pltpu.make_async_copy(flow.at[pl.ds(size * j, size), :], held.at[j], sems.at[j])

    for j in range(BLOCKS):
        fetch(j).start()
    wide = lax.broadcasted_iota(jnp.int32, (RZ, 128), 1) // RV == lax.broadcasted_iota(jnp.int32, (RZ, 128), 0)
    z_wide = lax.dot_general(z_ref[...], wide.astype(jnp.bfloat16), TN, preferred_element_type=jnp.float32)
    wide = lax.broadcasted_iota(jnp.int32, (RV, 128), 1) % RV == lax.broadcasted_iota(jnp.int32, (RV, 128), 0)
    v_wide = lax.dot_general(v_ref[...], wide.astype(jnp.bfloat16), TN, preferred_element_type=jnp.float32)
    for i in range(NZ):
        table[NV * i : NV * i + NV, :] = (z_wide[i : i + 1, :] * v_wide).astype(jnp.bfloat16)
    half = y_ref[pl.ds(pl.multiple_of(where_ref[0] * 16, 16), 16), :].astype(jnp.float32)
    for p in range(32):
        out_ref[p * 48 + 32 : p * 48 + 48, :] = half
    for i in range(BLOCKS):
        fetch(i).wait()
        block = lax.dot_general(held[i], table[...], NN, preferred_element_type=jnp.float32)
        for part in range(size // 128):
            j = i * (size // 128) + part
            turned[...] = block[part * 128 : part * 128 + 128, :].T.astype(jnp.bfloat16).astype(jnp.float32)
            for k in range(4):
                out_ref[pl.ds(k * 8 + j, 32, stride=48), :] = turned[pl.ds(k, 32, stride=4), :]


def reduced_blocks(where, flow, y_factor, z_factor, v_factor):
    return pl.pallas_call(
        reduced_kernel,
        out_shape=jax.ShapeDtypeStruct((32 * 48, 128), jnp.float32),
        in_specs=[pl.BlockSpec(memory_space=pltpu.SMEM), pl.BlockSpec(memory_space=pl.ANY)]
        + [pl.BlockSpec(memory_space=pltpu.VMEM)] * 3,
        out_specs=pl.BlockSpec(memory_space=pltpu.VMEM),
        scratch_shapes=[
            pltpu.VMEM((BLOCKS, 1024 // BLOCKS, NZ * NV), jnp.bfloat16),
            pltpu.VMEM((NZ * NV, 128), jnp.bfloat16),
            pltpu.VMEM((128, 128), jnp.float32),
            pltpu.SemaphoreType.DMA((BLOCKS,)),
        ],
        compiler_params=pltpu.CompilerParams(vmem_limit_bytes=56 * 1024 * 1024),
        name="reduced_blocks",
    )(where, flow, y_factor, z_factor, v_factor)


def projected_kernel(got, out_ref, ordered):
    quarter = lax.broadcasted_iota(jnp.int32, (64, 128), 1) // 32
    total = jnp.zeros((256, 128), jnp.float32)
    for gy in range(0, 16, 2):
        rows, table = [], []
        for g in (gy, gy + 1):
            low, high = g * 48, (16 + g) * 48
            block = jnp.concatenate([got[low : low + 32, :], got[high : high + 32, :]], axis=0)
            rows.append(
                jnp.concatenate([jnp.where(quarter == a, block, 0.0) for a in range(4)], axis=0)
            )
            factor = jnp.concatenate([got[low + 32 : low + 48, :], got[high + 32 : high + 48, :]], axis=0)
            table += [factor] * 4
        rows = jnp.concatenate(rows, axis=1).astype(jnp.bfloat16)
        table = jnp.concatenate(table, axis=0).astype(jnp.bfloat16)
        total = total + lax.dot_general(rows, table, NN, preferred_element_type=jnp.float32)
    for a in range(4):
        for h in range(2):
            for k in range(4):
                base = a * 64 + h * 32 + k * 8
                ordered[pl.ds(k * 64 + h * 32 + a, 8, stride=4), :] = total[base : base + 8, :]
    for k in range(4):
        out_ref[:, k * 128 : k * 128 + 128] = ordered[k * 64 : k * 64 + 64, :]


def projected_rows(got):
    return pl.pallas_call(
        projected_kernel,
        out_shape=jax.ShapeDtypeStruct((64, 512), jnp.float32),
        in_specs=[pl.BlockSpec(memory_space=pltpu.VMEM)],
        out_specs=pl.BlockSpec(memory_space=pltpu.VMEM),
        scratch_shapes=[pltpu.VMEM((256, 128), jnp.float32)],
        compiler_params=pltpu.CompilerParams(vmem_limit_bytes=16 * 1024 * 1024),
        name="projected_rows",
    )(got)


def strips_kernel(where_ref, *refs):
    blocks, out_ref = refs[:9], refs[9]
    odd = lax.rem(where_ref[0], 2)
    for t in range(4):
        near = blocks[4 + t][...]
        if t == 0:
            near = near * 0.5
        far = blocks[5 + t][...]
        swap = odd != (t % 2)
        pair = jnp.concatenate([jnp.where(swap, far, near), jnp.where(swap, near, far)], axis=0)
        tile = dot(blocks[4 - t][...], pair, NT)
        for g in range(8):
            out_ref[t * 8 + g, 0:8, :] = tile[8 * g : 8 * g + 8, :]
    last = dot(blocks[0][...], blocks[8][...], NT)
    last = jnp.concatenate([last[:32, :], last[32:, :]], axis=1)
    for p in range(32):
        out_ref[p, 8:16, :] = jnp.broadcast_to(last[p : p + 1, :], (8, 128))


def strips(z, blocks):
    return pl.pallas_call(
        strips_kernel,
        out_shape=jax.ShapeDtypeStruct((32, 16, 128), jnp.float32),
        in_specs=[pl.BlockSpec(memory_space=pltpu.SMEM)]
        + [pl.BlockSpec(memory_space=pltpu.VMEM)] * 9,
        out_specs=pl.BlockSpec(memory_space=pltpu.VMEM),
        compiler_params=pltpu.CompilerParams(vmem_limit_bytes=24 * 1024 * 1024),
        name="strips",
    )(z.reshape(1), *blocks)


def inverse_lower(correlation):
    full = (8, 128)
    sub = lax.broadcasted_iota(jnp.int32, full, 0)
    lane = lax.broadcasted_iota(jnp.int32, full, 1)

    def row(x, i):
        return jnp.broadcast_to(x[i : i + 1, :], full)

    def column(x, j):
        return jnp.broadcast_to(x[:, j : j + 1], full)

    def total(t):
        return ((t[0] + t[1]) + (t[2] + t[3])) + ((t[4] + t[5]) + (t[6] + t[7]))

    left = [correlation[8 * v : 8 * v + 8, :] for v in range(16)]
    eye = [lane == sub + 8 * v for v in range(16)]
    on = [jnp.where(eye[v], left[v], 0.0) for v in range(16)]
    acc = on[0]
    for v in range(1, 16):
        acc = acc + on[v]
    across = lax.rsqrt(jnp.broadcast_to(jnp.sum(acc, axis=0, keepdims=True), full))
    down = [lax.rsqrt(jnp.broadcast_to(jnp.sum(on[v], axis=1, keepdims=True), full)) for v in range(16)]
    left = [left[v] * across * down[v] for v in range(16)]
    right = [jnp.where(eye[v], across, 0.0) for v in range(16)]
    done = []
    for v in range(16):
        small = [column(left[v], 8 * v + i) for i in range(8)]
        rest, made = left[v], right[v]
        finished = jnp.zeros(full, jnp.float32)
        for i in (0, 2, 4, 6):
            j = i + 1
            a, b, d = row(small[i], i), row(small[i], j), row(small[j], j)
            inverse = 1.0 / (a * d - b * b)
            ia, ib, id_ = d * inverse, b * inverse, a * inverse
            at_i, at_j = sub == i, sub == j
            here = jnp.logical_or(at_i, at_j)
            share_i = jnp.where(at_i, -ia, jnp.where(at_j, ib, small[i] * ia - small[j] * ib))
            share_j = jnp.where(at_i, ib, jnp.where(at_j, -id_, small[j] * id_ - small[i] * ib))
            made_i, made_j = row(made, i), row(made, j)
            root = lax.rsqrt(a)
            root = root * (1.5 - 0.5 * a * root * root)
            ratio = b * root * root
            left_over = d - b * ratio
            second = lax.rsqrt(left_over)
            second = second * (1.5 - 0.5 * left_over * second * second)
            finished = jnp.where(at_i, made_i * root, jnp.where(at_j, (made_j - ratio * made_i) * second, finished))
            def less(x, x_i, x_j):
                return jnp.where(here, 0.0, x) - (share_i * x_i + share_j * x_j)
            made = less(made, made_i, made_j)
            if v < 15:
                rest = less(rest, row(rest, i), row(rest, j))
            for k in range(i + 2, 8):
                small[k] = less(small[k], row(small[k], i), row(small[k], j))
        done.append(finished)
        if v < 15:
            rest_rows = [row(rest, i) for i in range(8)]
            made_rows = [row(made, i) for i in range(8)]
            for w in range(v + 1, 16):
                shares = [column(left[w], 8 * v + i) for i in range(8)]
                left[w] = left[w] - total([shares[i] * rest_rows[i] for i in range(8)])
                right[w] = right[w] - total([shares[i] * made_rows[i] for i in range(8)])
    return jnp.concatenate(done, axis=0)


def sweeps_kernel(where_ref, mine, other, rows_ref, cols_ref, parts, half, far, start, basis, sems):
    z, h, c = where_ref[0], where_ref[1], where_ref[2]
    first = pltpu.make_async_copy(mine, parts.at[c], sems.at[0])
    second = pltpu.make_async_copy(other, parts.at[1 - c], sems.at[1])
    first.start()
    second.start()
    first.wait()
    second.wait()
    lower_lanes = lax.broadcasted_iota(jnp.int32, (8, 128), 1) < 64

    for zz in range(16):
        for hh in range(2):
            for cc in range(2):
                for e in range(2):
                    start[pl.ds(zz * 64 + hh * 32 + 2 * cc + e, 8, stride=4), :] = parts[
                        cc, pl.ds(hh * 8 * PART + 136 + 2 * zz + e, 8, stride=PART), :
                    ]
    for zz in range(16):
        basis[:, zz * 64 : zz * 64 + 64] = start[zz * 64 : zz * 64 + 64, :].T

    for zz in range(8):
        for cc in range(2):
            for g in range(2):
                far[pl.ds(zz * 32 + cc + 16 * g, 8, stride=2), :] = parts[
                    cc, pl.ds(g * 8 * PART + 128 + zz, 8, stride=PART), :
                ]

    def source(row_z, col_z, g):
        d = (col_z - row_z) % 16
        z_of = (row_z + d // 2) % 16
        if d < 8:
            p = (d // 2) * 8 + g
            base = (p // 2) * PART + z_of * 8
            return parts[p % 2, base : base + 8, :]
        if d == 8 and z_of < 8:
            block = far[z_of * 32 + (g % 4) * 8 : z_of * 32 + (g % 4) * 8 + 8, :]
            if (g >= 4) != (col_z % 2 == 1):
                block = pltpu.roll(block, 64, 1)
            return block
        return jnp.zeros((8, 128), jnp.float32)

    for row_z in range(16):
        for pair in range(8):
            for g in range(8):
                a = source(row_z, 2 * pair, g)
                b = source(row_z, 2 * pair + 1, g)
                half[row_z * 64 + g * 8 : row_z * 64 + g * 8 + 8, pair * 128 : pair * 128 + 128] = (
                    jnp.where(lower_lanes, a, b)
                )
    for i in range(8):
        for j in range(i + 1):
            rows, cols = slice(i * 128, i * 128 + 128), slice(j * 128, j * 128 + 128)
            block = half[rows, cols] + half[cols, rows].T
            half[rows, cols] = block
            if i != j:
                half[cols, rows] = block.T

    def sweep(_, carry):
        image = dot(basis[...], half[...], NN)
        correlation = dot(image, image, NT)
        basis[...] = dot(inverse_lower(correlation), image, NN)
        return carry

    lax.fori_loop(0, ITERS, sweep, 0)
    pick = lax.broadcasted_iota(jnp.int32, (32, 1024), 1) == (
        lax.broadcasted_iota(jnp.int32, (32, 1024), 0) + (z * 2 + h) * 32
    )
    rows_ref[...] = dot(jnp.where(pick, 1.0, 0.0), basis[...], NT)
    cols_ref[...] = basis[pl.ds(pl.multiple_of(z * 8, 8), 8), :]


def core_kernel(cols_ref, every_ref, core_ref):
    core_ref[...] = dot(cols_ref[...], every_ref[...], NN)


def core_rows(cols, every):
    return pl.pallas_call(
        core_kernel,
        out_shape=jax.ShapeDtypeStruct((8, 512), jnp.float32),
        in_specs=[pl.BlockSpec(memory_space=pltpu.VMEM)] * 2,
        out_specs=pl.BlockSpec(memory_space=pltpu.VMEM),
        compiler_params=pltpu.CompilerParams(vmem_limit_bytes=16 * 1024 * 1024),
        name="core_rows",
    )(cols, every)


def sweeps(where, mine, other):
    return pl.pallas_call(
        sweeps_kernel,
        out_shape=(
            jax.ShapeDtypeStruct((32, RX), jnp.float32),
            jax.ShapeDtypeStruct((8, 1024), jnp.float32),
        ),
        in_specs=[
            pl.BlockSpec(memory_space=pltpu.SMEM),
            pl.BlockSpec(memory_space=pl.ANY),
            pl.BlockSpec(memory_space=pl.ANY),
        ],
        out_specs=[pl.BlockSpec(memory_space=pltpu.VMEM)] * 2,
        scratch_shapes=[
            pltpu.VMEM((2, 16 * PART, 128), jnp.float32),
            pltpu.VMEM((1024, 1024), jnp.float32),
            pltpu.VMEM((8 * 32, 128), jnp.float32),
            pltpu.VMEM((1024, 128), jnp.float32),
            pltpu.VMEM((128, 1024), jnp.float32),
            pltpu.SemaphoreType.DMA((2,)),
        ],
        compiler_params=pltpu.CompilerParams(vmem_limit_bytes=32 * 1024 * 1024),
        name="sweeps",
    )(where, mine, other)


def local(flow_field, y_factor, z_factor, v_factor, x_start):
    z = lax.axis_index("z").astype(jnp.int32)
    h = lax.axis_index("h").astype(jnp.int32)
    c = lax.axis_index("c").astype(jnp.int32)
    send = reduced_blocks(
        h.reshape(1), flow_field.reshape(1024, NZ * NV), y_factor, z_factor.T, v_factor.T
    )
    got = lax.all_to_all(send.reshape(32, 48, 128), PLANE, 0, 0)
    projected = projected_rows(got.reshape(32 * 48, 128))

    def from_z(block, distance):
        return lax.ppermute(block, "z", [(i, (i - distance) % 16) for i in range(16)])

    near = {d: from_z(projected, d) for d in (2, -2, 1, -1)}
    for sign in (1, -1):
        pair = from_z(jnp.concatenate([near[sign], near[2 * sign]], axis=0), 2 * sign)
        near[3 * sign], near[4 * sign] = pair[:64], pair[64:]
    near[0] = projected
    blocks = [near[d] for d in range(-4, 5)]
    tied, *_ = lax.optimization_barrier((projected, near[4], near[-4]))
    every = lax.all_gather(tied, "z").reshape(1024, 512)

    part = lax.all_to_all(strips(z, blocks), PLANE, 0, 0).sum(0)
    gy = (lax.axis_index("y") * 4 + lax.axis_index("l") * 2 + c).astype(jnp.int32)
    start = lax.dynamic_slice_in_dim(x_start, 2 * gy, 2, 0)
    part = jnp.concatenate([part[:9], start, jnp.zeros((5, 128), jnp.float32)], axis=0)
    line = lax.all_gather(part, "z")
    line = jnp.concatenate(
        [line[:, :8].reshape(128, 128), line[:8, 8], line[:, 9:11].reshape(32, 128)], axis=0
    )
    mine = lax.all_to_all(jnp.broadcast_to(line[None], (16, PART, 128)), XY, 0, 0)
    mine = mine.reshape(16 * PART, 128)
    other = lax.ppermute(mine, "c", [(0, 1), (1, 0)])

    x_factor, cols = sweeps(jnp.stack([z, h, c]), mine, other)
    core = core_rows(cols, every)
    core = core.reshape(2, 4, 4, 16, 8).transpose(0, 3, 1, 2, 4).reshape(32, 1, 128)
    core = lax.all_to_all(core, PLANE, 0, 0).reshape(32, 4, 4, 8)
    core = core.transpose(1, 3, 0, 2).reshape(4, 1024)
    return (x_factor, core)


def solution(mesh):
    fine = Mesh(mesh.devices.reshape(16, 2, 4, 2, 2), ("z", "h", "y", "l", "c"))
    gx, gy = ("z", "h"), ("y", "l", "c")
    placed = (P(gx, gy, None), P(gy, None), P(), P(), P(gx, None))
    return jax.shard_map(
        local, mesh=fine, in_specs=placed, out_specs=(P(gx, None), P(gx, gy)), check_vma=False
    )
```

```python
import jax
import jax.numpy as jnp
from jax import lax
from jax.experimental import pallas as pl
from jax.experimental.pallas import tpu as pltpu
from jax.sharding import Mesh, PartitionSpec as P

NZ = 64
NV = 32
RX = 128
RY = 128
RZ = 16
RV = 8
ITERS = 3
HIGHEST = lax.Precision.HIGHEST
PLANE = ("h", "y", "l", "c")
XY = ("h", "y", "l")
PART = 168
NN = (((1,), (0,)), ((), ()))
NT = (((1,), (1,)), ((), ()))
TN = (((0,), (0,)), ((), ()))
BLOCKS = 4


def dot(a, b, dims):
    return lax.dot_general(a, b, dims, precision=HIGHEST, preferred_element_type=jnp.float32)


def reduced_kernel(where_ref, flow, y_ref, z_ref, v_ref, out_ref, held, table, turned, sems):
    size = 1024 // BLOCKS

    def fetch(j):
        return pltpu.make_async_copy(flow.at[pl.ds(size * j, size), :], held.at[j], sems.at[j])

    for j in range(BLOCKS):
        fetch(j).start()
    wide = lax.broadcasted_iota(jnp.int32, (RZ, 128), 1) // RV == lax.broadcasted_iota(jnp.int32, (RZ, 128), 0)
    z_wide = lax.dot_general(z_ref[...], wide.astype(jnp.bfloat16), TN, preferred_element_type=jnp.float32)
    wide = lax.broadcasted_iota(jnp.int32, (RV, 128), 1) % RV == lax.broadcasted_iota(jnp.int32, (RV, 128), 0)
    v_wide = lax.dot_general(v_ref[...], wide.astype(jnp.bfloat16), TN, preferred_element_type=jnp.float32)
    for i in range(NZ):
        table[NV * i : NV * i + NV, :] = (z_wide[i : i + 1, :] * v_wide).astype(jnp.bfloat16)
    half = y_ref[pl.ds(pl.multiple_of(where_ref[0] * 16, 16), 16), :].astype(jnp.float32)
    for p in range(32):
        out_ref[p * 48 + 32 : p * 48 + 48, :] = half
    for i in range(BLOCKS):
        fetch(i).wait()
        block = lax.dot_general(held[i], table[...], NN, preferred_element_type=jnp.float32)
        for part in range(size // 128):
            j = i * (size // 128) + part
            turned[...] = block[part * 128 : part * 128 + 128, :].T.astype(jnp.bfloat16).astype(jnp.float32)
            for k in range(4):
                out_ref[pl.ds(k * 8 + j, 32, stride=48), :] = turned[pl.ds(k, 32, stride=4), :]


def reduced_blocks(where, flow, y_factor, z_factor, v_factor):
    return pl.pallas_call(
        reduced_kernel,
        out_shape=jax.ShapeDtypeStruct((32 * 48, 128), jnp.float32),
        in_specs=[pl.BlockSpec(memory_space=pltpu.SMEM), pl.BlockSpec(memory_space=pl.ANY)]
        + [pl.BlockSpec(memory_space=pltpu.VMEM)] * 3,
        out_specs=pl.BlockSpec(memory_space=pltpu.VMEM),
        scratch_shapes=[
            pltpu.VMEM((BLOCKS, 1024 // BLOCKS, NZ * NV), jnp.bfloat16),
            pltpu.VMEM((NZ * NV, 128), jnp.bfloat16),
            pltpu.VMEM((128, 128), jnp.float32),
            pltpu.SemaphoreType.DMA((BLOCKS,)),
        ],
        compiler_params=pltpu.CompilerParams(vmem_limit_bytes=56 * 1024 * 1024),
        name="reduced_blocks",
    )(where, flow, y_factor, z_factor, v_factor)


def projected_kernel(got, out_ref, own_ref, ordered):
    quarter = lax.broadcasted_iota(jnp.int32, (64, 128), 1) // 32
    total = jnp.zeros((256, 128), jnp.float32)
    for gy in range(0, 16, 2):
        rows, table = [], []
        for g in (gy, gy + 1):
            low, high = g * 48, (16 + g) * 48
            block = jnp.concatenate([got[low : low + 32, :], got[high : high + 32, :]], axis=0)
            rows.append(
                jnp.concatenate([jnp.where(quarter == a, block, 0.0) for a in range(4)], axis=0)
            )
            factor = jnp.concatenate([got[low + 32 : low + 48, :], got[high + 32 : high + 48, :]], axis=0)
            table += [factor] * 4
        rows = jnp.concatenate(rows, axis=1).astype(jnp.bfloat16)
        table = jnp.concatenate(table, axis=0).astype(jnp.bfloat16)
        total = total + lax.dot_general(rows, table, NN, preferred_element_type=jnp.float32)
    for a in range(4):
        for h in range(2):
            for k in range(4):
                base = a * 64 + h * 32 + k * 8
                ordered[pl.ds(k * 64 + h * 32 + a, 8, stride=4), :] = total[base : base + 8, :]
    for k in range(4):
        out_ref[:, k * 128 : k * 128 + 128] = ordered[k * 64 : k * 64 + 64, :]
        own_ref[:, k * 128 : k * 128 + 128] = ordered[k * 64 : k * 64 + 64, :]


def projected_rows(got):
    return pl.pallas_call(
        projected_kernel,
        out_shape=(jax.ShapeDtypeStruct((64, 512), jnp.float32),) * 2,
        in_specs=[pl.BlockSpec(memory_space=pltpu.VMEM)],
        out_specs=[pl.BlockSpec(memory_space=pltpu.VMEM)] * 2,
        scratch_shapes=[pltpu.VMEM((256, 128), jnp.float32)],
        compiler_params=pltpu.CompilerParams(vmem_limit_bytes=16 * 1024 * 1024),
        name="projected_rows",
    )(got)


def strips_kernel(where_ref, *refs):
    blocks, out_ref = refs[:9], refs[9]
    odd = lax.rem(where_ref[0], 2)
    for t in range(4):
        near = blocks[4 + t][...]
        if t == 0:
            near = near * 0.5
        far = blocks[5 + t][...]
        swap = odd != (t % 2)
        pair = jnp.concatenate([jnp.where(swap, far, near), jnp.where(swap, near, far)], axis=0)
        tile = dot(blocks[4 - t][...], pair, NT)
        for g in range(8):
            out_ref[t * 8 + g, 0:8, :] = tile[8 * g : 8 * g + 8, :]
    last = dot(blocks[0][...], blocks[8][...], NT)
    last = jnp.concatenate([last[:32, :], last[32:, :]], axis=1)
    for p in range(32):
        out_ref[p, 8:16, :] = jnp.broadcast_to(last[p : p + 1, :], (8, 128))


def strips(z, blocks):
    return pl.pallas_call(
        strips_kernel,
        out_shape=jax.ShapeDtypeStruct((32, 16, 128), jnp.float32),
        in_specs=[pl.BlockSpec(memory_space=pltpu.SMEM)]
        + [pl.BlockSpec(memory_space=pltpu.VMEM)] * 9,
        out_specs=pl.BlockSpec(memory_space=pltpu.VMEM),
        compiler_params=pltpu.CompilerParams(vmem_limit_bytes=16 * 1024 * 1024),
        name="strips",
    )(z.reshape(1), *blocks)


def inverse_lower(correlation):
    full = (8, 128)
    sub = lax.broadcasted_iota(jnp.int32, full, 0)
    lane = lax.broadcasted_iota(jnp.int32, full, 1)
    left = [correlation[8 * v : 8 * v + 8, :] for v in range(16)]
    right = [jnp.where(lane == sub + 8 * v, 1.0, 0.0) for v in range(16)]
    done = []

    def row(x, i):
        return jnp.broadcast_to(x[i : i + 1, :], full)

    def column(x, j):
        return jnp.broadcast_to(x[:, j : j + 1], full)

    for v in range(16):
        small = [column(left[v], 8 * v + i) for i in range(8)]
        rest, made = left[v], right[v]
        finished = jnp.zeros(full, jnp.float32)
        for i in range(8):
            pivot = row(small[i], i)
            inverse = 1.0 / pivot
            here = sub == i
            share = jnp.where(here, -inverse, small[i] * inverse)
            made_row = row(made, i)
            root = lax.rsqrt(pivot)
            root = root * (1.5 - 0.5 * pivot * root * root)
            finished = jnp.where(here, made_row * root, finished)
            made = jnp.where(here, 0.0, made) - share * made_row
            if v < 15:
                rest = jnp.where(here, 0.0, rest) - share * row(rest, i)
            for k in range(i + 1, 8):
                small[k] = jnp.where(here, 0.0, small[k]) - share * row(small[k], i)
        done.append(finished)
        if v < 15:
            rest_rows = [row(rest, i) for i in range(8)]
            made_rows = [row(made, i) for i in range(8)]
            for w in range(v + 1, 16):
                shares = [column(left[w], 8 * v + i) for i in range(8)]
                taken = [shares[i] * rest_rows[i] for i in range(8)]
                left[w] = left[w] - (
                    ((taken[0] + taken[1]) + (taken[2] + taken[3]))
                    + ((taken[4] + taken[5]) + (taken[6] + taken[7]))
                )
                taken = [shares[i] * made_rows[i] for i in range(8)]
                right[w] = right[w] - (
                    ((taken[0] + taken[1]) + (taken[2] + taken[3]))
                    + ((taken[4] + taken[5]) + (taken[6] + taken[7]))
                )
    return jnp.concatenate(done, axis=0)


def sweeps_kernel(where_ref, mine, other, rows_ref, cols_ref, parts, half, far, start, basis, sems):
    z, h, c = where_ref[0], where_ref[1], where_ref[2]
    first = pltpu.make_async_copy(mine, parts.at[c], sems.at[0])
    second = pltpu.make_async_copy(other, parts.at[1 - c], sems.at[1])
    first.start()
    second.start()
    first.wait()
    second.wait()
    lower_lanes = lax.broadcasted_iota(jnp.int32, (8, 128), 1) < 64

    for zz in range(16):
        for hh in range(2):
            for cc in range(2):
                for e in range(2):
                    start[pl.ds(zz * 64 + hh * 32 + 2 * cc + e, 8, stride=4), :] = parts[
                        cc, pl.ds(hh * 8 * PART + 136 + 2 * zz + e, 8, stride=PART), :
                    ]
    for zz in range(16):
        basis[:, zz * 64 : zz * 64 + 64] = start[zz * 64 : zz * 64 + 64, :].T

    for zz in range(8):
        for cc in range(2):
            for g in range(2):
                far[pl.ds(zz * 32 + cc + 16 * g, 8, stride=2), :] = parts[
                    cc, pl.ds(g * 8 * PART + 128 + zz, 8, stride=PART), :
                ]

    def source(row_z, col_z, g):
        d = (col_z - row_z) % 16
        z_of = (row_z + d // 2) % 16
        if d < 8:
            p = (d // 2) * 8 + g
            base = (p // 2) * PART + z_of * 8
            return parts[p % 2, base : base + 8, :]
        if d == 8 and z_of < 8:
            block = far[z_of * 32 + (g % 4) * 8 : z_of * 32 + (g % 4) * 8 + 8, :]
            if (g >= 4) != (col_z % 2 == 1):
                block = pltpu.roll(block, 64, 1)
            return block
        return jnp.zeros((8, 128), jnp.float32)

    for row_z in range(16):
        for pair in range(8):
            for g in range(8):
                a = source(row_z, 2 * pair, g)
                b = source(row_z, 2 * pair + 1, g)
                half[row_z * 64 + g * 8 : row_z * 64 + g * 8 + 8, pair * 128 : pair * 128 + 128] = (
                    jnp.where(lower_lanes, a, b)
                )
    for i in range(8):
        for j in range(i + 1):
            rows, cols = slice(i * 128, i * 128 + 128), slice(j * 128, j * 128 + 128)
            block = half[rows, cols] + half[cols, rows].T
            half[rows, cols] = block
            if i != j:
                half[cols, rows] = block.T

    def sweep(_, carry):
        image = dot(basis[...], half[...], NN)
        correlation = dot(image, image, NT)
        basis[...] = dot(inverse_lower(correlation), image, NN)
        return carry

    lax.fori_loop(0, ITERS, sweep, 0)
    pick = lax.broadcasted_iota(jnp.int32, (32, 1024), 1) == (
        lax.broadcasted_iota(jnp.int32, (32, 1024), 0) + (z * 2 + h) * 32
    )
    rows_ref[...] = dot(jnp.where(pick, 1.0, 0.0), basis[...], NT)
    cols_ref[...] = basis[pl.ds(pl.multiple_of(z * 8, 8), 8), :]


def core_kernel(cols_ref, every_ref, core_ref):
    core_ref[...] = dot(cols_ref[...], every_ref[...], NN)


def core_rows(cols, every):
    return pl.pallas_call(
        core_kernel,
        out_shape=jax.ShapeDtypeStruct((8, 512), jnp.float32),
        in_specs=[pl.BlockSpec(memory_space=pltpu.VMEM)] * 2,
        out_specs=pl.BlockSpec(memory_space=pltpu.VMEM),
        compiler_params=pltpu.CompilerParams(vmem_limit_bytes=16 * 1024 * 1024),
        name="core_rows",
    )(cols, every)


def sweeps(where, mine, other):
    return pl.pallas_call(
        sweeps_kernel,
        out_shape=(
            jax.ShapeDtypeStruct((32, RX), jnp.float32),
            jax.ShapeDtypeStruct((8, 1024), jnp.float32),
        ),
        in_specs=[
            pl.BlockSpec(memory_space=pltpu.SMEM),
            pl.BlockSpec(memory_space=pl.ANY),
            pl.BlockSpec(memory_space=pl.ANY),
        ],
        out_specs=[pl.BlockSpec(memory_space=pltpu.VMEM)] * 2,
        scratch_shapes=[
            pltpu.VMEM((2, 16 * PART, 128), jnp.float32),
            pltpu.VMEM((1024, 1024), jnp.float32),
            pltpu.VMEM((8 * 32, 128), jnp.float32),
            pltpu.VMEM((1024, 128), jnp.float32),
            pltpu.VMEM((128, 1024), jnp.float32),
            pltpu.SemaphoreType.DMA((2,)),
        ],
        compiler_params=pltpu.CompilerParams(vmem_limit_bytes=32 * 1024 * 1024),
        name="sweeps",
    )(where, mine, other)


def local(flow_field, y_factor, z_factor, v_factor, x_start):
    z = lax.axis_index("z").astype(jnp.int32)
    h = lax.axis_index("h").astype(jnp.int32)
    c = lax.axis_index("c").astype(jnp.int32)
    send = reduced_blocks(
        h.reshape(1), flow_field.reshape(1024, NZ * NV), y_factor, z_factor.T, v_factor.T
    )
    got = lax.all_to_all(send.reshape(32, 48, 128), PLANE, 0, 0)
    projected, own = projected_rows(got.reshape(32 * 48, 128))

    def from_z(block, distance):
        return lax.ppermute(block, "z", [(i, (i - distance) % 16) for i in range(16)])

    near = {d: from_z(projected, d) for d in (2, -2, 1, -1)}
    for sign in (1, -1):
        pair = from_z(jnp.concatenate([near[sign], near[2 * sign]], axis=0), 2 * sign)
        near[3 * sign], near[4 * sign] = pair[:64], pair[64:]
    near[0] = projected
    blocks = [near[d] for d in range(-4, 5)]

    own, *_ = lax.optimization_barrier((own, near[4], near[-4]))
    every = lax.all_gather(own, "z").reshape(1024, 512)

    part = lax.all_to_all(strips(z, blocks), PLANE, 0, 0).sum(0)
    gy = (lax.axis_index("y") * 4 + lax.axis_index("l") * 2 + c).astype(jnp.int32)
    start = lax.dynamic_slice_in_dim(x_start, 2 * gy, 2, 0)
    part = jnp.concatenate([part[:9], start, jnp.zeros((5, 128), jnp.float32)], axis=0)
    line = lax.all_to_all(jnp.broadcast_to(part[None], (16, 16, 128)), "z", 0, 0)
    line = jnp.concatenate(
        [line[:, :8].reshape(128, 128), line[:8, 8], line[:, 9:11].reshape(32, 128)], axis=0
    )
    mine = lax.all_to_all(jnp.broadcast_to(line[None], (16, PART, 128)), XY, 0, 0)
    mine = mine.reshape(16 * PART, 128)
    other = lax.ppermute(mine, "c", [(0, 1), (1, 0)])

    x_factor, cols = sweeps(jnp.stack([z, h, c]), mine, other)
    core = core_rows(cols, every)
    core = core.reshape(2, 4, 4, 16, 8).transpose(0, 3, 1, 2, 4).reshape(32, 1, 128)
    core = lax.all_to_all(core, PLANE, 0, 0).reshape(32, 4, 4, 8)
    core = core.transpose(1, 3, 0, 2).reshape(4, 1024)
    return (x_factor, core)


def solution(mesh):
    fine = Mesh(mesh.devices.reshape(16, 2, 4, 2, 2), ("z", "h", "y", "l", "c"))
    gx, gy = ("z", "h"), ("y", "l", "c")
    placed = (P(gx, gy, None), P(gy, None), P(), P(), P(gx, None))
    return jax.shard_map(
        local, mesh=fine, in_specs=placed, out_specs=(P(gx, None), P(gx, gy)), check_vma=False
    )
```

```python
import jax
import jax.numpy as jnp
from jax import lax
from jax.experimental import pallas as pl
from jax.experimental.pallas import tpu as pltpu
from jax.sharding import Mesh, PartitionSpec as P

NZ = 64
NV = 32
RX = 128
RY = 128
RZ = 16
RV = 8
ITERS = 3
HIGHEST = lax.Precision.HIGHEST
PLANE = ("h", "y", "l", "c")
XY = ("h", "y", "l")
PART = 168
NN = (((1,), (0,)), ((), ()))
NT = (((1,), (1,)), ((), ()))
TN = (((0,), (0,)), ((), ()))
BLOCKS = 4


def dot(a, b, dims):
    return lax.dot_general(a, b, dims, precision=HIGHEST, preferred_element_type=jnp.float32)


def reduced_kernel(where_ref, flow, small_ref, out_ref, held, table, turned, sems):
    size = 1024 // BLOCKS

    def fetch(j):
        return pltpu.make_async_copy(flow.at[pl.ds(size * j, size), :], held.at[j], sems.at[j])

    for j in range(BLOCKS):
        fetch(j).start()
    wide = lax.broadcasted_iota(jnp.int32, (16, 128), 1) // RV == lax.broadcasted_iota(jnp.int32, (16, 128), 0)
    z_wide = lax.dot_general(
        small_ref[32:48, :], wide.astype(jnp.bfloat16), TN, preferred_element_type=jnp.float32
    )
    wide = lax.broadcasted_iota(jnp.int32, (16, 128), 1) % RV == lax.broadcasted_iota(jnp.int32, (16, 128), 0)
    v_wide = lax.dot_general(
        small_ref[48:64, :], wide.astype(jnp.bfloat16), TN, preferred_element_type=jnp.float32
    )[:NV, :]
    for i in range(NZ):
        table[NV * i : NV * i + NV, :] = (z_wide[i : i + 1, :] * v_wide).astype(jnp.bfloat16)
    half = small_ref[pl.ds(pl.multiple_of(where_ref[0] * 16, 16), 16), :].astype(jnp.float32)
    for p in range(32):
        out_ref[p * 48 + 32 : p * 48 + 48, :] = half
    for i in range(BLOCKS):
        fetch(i).wait()
        block = lax.dot_general(held[i], table[...], NN, preferred_element_type=jnp.float32)
        for part in range(size // 128):
            j = i * (size // 128) + part
            turned[...] = block[part * 128 : part * 128 + 128, :].T.astype(jnp.bfloat16).astype(jnp.float32)
            for k in range(4):
                out_ref[pl.ds(k * 8 + j, 32, stride=48), :] = turned[pl.ds(k, 32, stride=4), :]


def reduced_blocks(where, flow, y_factor, z_factor, v_factor):
    small = jnp.concatenate(
        [
            y_factor,
            jnp.pad(z_factor.T, ((0, 0), (0, 128 - NZ))),
            jnp.pad(v_factor.T, ((0, 16 - RV), (0, 128 - NV))),
        ],
        axis=0,
    )
    return pl.pallas_call(
        reduced_kernel,
        out_shape=jax.ShapeDtypeStruct((32 * 48, 128), jnp.float32),
        in_specs=[pl.BlockSpec(memory_space=pltpu.SMEM), pl.BlockSpec(memory_space=pl.ANY)]
        + [pl.BlockSpec(memory_space=pltpu.VMEM)],
        out_specs=pl.BlockSpec(memory_space=pltpu.VMEM),
        scratch_shapes=[
            pltpu.VMEM((BLOCKS, 1024 // BLOCKS, NZ * NV), jnp.bfloat16),
            pltpu.VMEM((NZ * NV, 128), jnp.bfloat16),
            pltpu.VMEM((128, 128), jnp.float32),
            pltpu.SemaphoreType.DMA((BLOCKS,)),
        ],
        compiler_params=pltpu.CompilerParams(vmem_limit_bytes=53 * 1024 * 1024),
        name="reduced_blocks",
    )(where, flow, small)


def projected_kernel(got, out_ref, own_ref, ordered):
    quarter = lax.broadcasted_iota(jnp.int32, (64, 128), 1) // 32
    total = jnp.zeros((256, 128), jnp.float32)
    for gy in range(0, 16, 2):
        rows, table = [], []
        for g in (gy, gy + 1):
            low, high = g * 48, (16 + g) * 48
            block = jnp.concatenate([got[low : low + 32, :], got[high : high + 32, :]], axis=0)
            rows.append(
                jnp.concatenate([jnp.where(quarter == a, block, 0.0) for a in range(4)], axis=0)
            )
            factor = jnp.concatenate([got[low + 32 : low + 48, :], got[high + 32 : high + 48, :]], axis=0)
            table += [factor] * 4
        rows = jnp.concatenate(rows, axis=1).astype(jnp.bfloat16)
        table = jnp.concatenate(table, axis=0).astype(jnp.bfloat16)
        total = total + lax.dot_general(rows, table, NN, preferred_element_type=jnp.float32)
    for a in range(4):
        for h in range(2):
            for k in range(4):
                base = a * 64 + h * 32 + k * 8
                ordered[pl.ds(k * 64 + h * 32 + a, 8, stride=4), :] = total[base : base + 8, :]
    for k in range(4):
        out_ref[:, k * 128 : k * 128 + 128] = ordered[k * 64 : k * 64 + 64, :]
        own_ref[:, k * 128 : k * 128 + 128] = ordered[k * 64 : k * 64 + 64, :]


def projected_rows(got):
    return pl.pallas_call(
        projected_kernel,
        out_shape=(jax.ShapeDtypeStruct((64, 512), jnp.float32),) * 2,
        in_specs=[pl.BlockSpec(memory_space=pltpu.VMEM)],
        out_specs=[pl.BlockSpec(memory_space=pltpu.VMEM)] * 2,
        scratch_shapes=[pltpu.VMEM((256, 128), jnp.float32)],
        compiler_params=pltpu.CompilerParams(vmem_limit_bytes=16 * 1024 * 1024),
        name="projected_rows",
    )(got)


def strips_kernel(where_ref, *refs):
    blocks, out_ref = refs[:9], refs[9]
    odd = lax.rem(where_ref[0], 2)
    for t in range(4):
        near = blocks[4 + t][...]
        if t == 0:
            near = near * 0.5
        far = blocks[5 + t][...]
        swap = odd != (t % 2)
        pair = jnp.concatenate([jnp.where(swap, far, near), jnp.where(swap, near, far)], axis=0)
        tile = dot(blocks[4 - t][...], pair, NT)
        for g in range(8):
            out_ref[t * 8 + g, 0:8, :] = tile[8 * g : 8 * g + 8, :]
    last = dot(blocks[0][...], blocks[8][...], NT)
    last = jnp.concatenate([last[:32, :], last[32:, :]], axis=1)
    for p in range(32):
        out_ref[p, 8:16, :] = jnp.broadcast_to(last[p : p + 1, :], (8, 128))


def strips(z, blocks):
    return pl.pallas_call(
        strips_kernel,
        out_shape=jax.ShapeDtypeStruct((32, 16, 128), jnp.float32),
        in_specs=[pl.BlockSpec(memory_space=pltpu.SMEM)]
        + [pl.BlockSpec(memory_space=pltpu.VMEM)] * 9,
        out_specs=pl.BlockSpec(memory_space=pltpu.VMEM),
        compiler_params=pltpu.CompilerParams(vmem_limit_bytes=16 * 1024 * 1024),
        name="strips",
    )(z.reshape(1), *blocks)


def inverse_lower(correlation):
    full = (8, 128)
    sub = lax.broadcasted_iota(jnp.int32, full, 0)
    lane = lax.broadcasted_iota(jnp.int32, full, 1)
    left = [correlation[8 * v : 8 * v + 8, :] for v in range(16)]
    right = [jnp.where(lane == sub + 8 * v, 1.0, 0.0) for v in range(16)]
    done = []

    def row(x, i):
        return jnp.broadcast_to(x[i : i + 1, :], full)

    def column(x, j):
        return jnp.broadcast_to(x[:, j : j + 1], full)

    for v in range(16):
        small = [column(left[v], 8 * v + i) for i in range(8)]
        rest, made = left[v], right[v]
        finished = jnp.zeros(full, jnp.float32)
        for i in range(8):
            pivot = row(small[i], i)
            inverse = 1.0 / pivot
            here = sub == i
            share = jnp.where(here, -inverse, small[i] * inverse)
            made_row = row(made, i)
            root = lax.rsqrt(pivot)
            root = root * (1.5 - 0.5 * pivot * root * root)
            finished = jnp.where(here, made_row * root, finished)
            made = jnp.where(here, 0.0, made) - share * made_row
            if v < 15:
                rest = jnp.where(here, 0.0, rest) - share * row(rest, i)
            for k in range(i + 1, 8):
                small[k] = jnp.where(here, 0.0, small[k]) - share * row(small[k], i)
        done.append(finished)
        if v < 15:
            rest_rows = [row(rest, i) for i in range(8)]
            made_rows = [row(made, i) for i in range(8)]
            for w in range(v + 1, 16):
                shares = [column(left[w], 8 * v + i) for i in range(8)]
                taken = [shares[i] * rest_rows[i] for i in range(8)]
                left[w] = left[w] - (
                    ((taken[0] + taken[1]) + (taken[2] + taken[3]))
                    + ((taken[4] + taken[5]) + (taken[6] + taken[7]))
                )
                taken = [shares[i] * made_rows[i] for i in range(8)]
                right[w] = right[w] - (
                    ((taken[0] + taken[1]) + (taken[2] + taken[3]))
                    + ((taken[4] + taken[5]) + (taken[6] + taken[7]))
                )
    return jnp.concatenate(done, axis=0)


def assemble(parts, half, far, start, basis):
    lower_lanes = lax.broadcasted_iota(jnp.int32, (8, 128), 1) < 64

    for zz in range(16):
        for hh in range(2):
            for cc in range(2):
                for e in range(2):
                    start[pl.ds(zz * 64 + hh * 32 + 2 * cc + e, 8, stride=4), :] = parts[cc][
                        pl.ds(hh * 8 * PART + 136 + 2 * zz + e, 8, stride=PART), :
                    ]
    for zz in range(16):
        basis[:, zz * 64 : zz * 64 + 64] = start[zz * 64 : zz * 64 + 64, :].T

    for zz in range(8):
        for cc in range(2):
            for g in range(2):
                far[pl.ds(zz * 32 + cc + 16 * g, 8, stride=2), :] = parts[cc][
                    pl.ds(g * 8 * PART + 128 + zz, 8, stride=PART), :
                ]

    def source(row_z, col_z, g):
        d = (col_z - row_z) % 16
        z_of = (row_z + d // 2) % 16
        if d < 8:
            p = (d // 2) * 8 + g
            base = (p // 2) * PART + z_of * 8
            return parts[p % 2][base : base + 8, :]
        if d == 8 and z_of < 8:
            block = far[z_of * 32 + (g % 4) * 8 : z_of * 32 + (g % 4) * 8 + 8, :]
            if (g >= 4) != (col_z % 2 == 1):
                block = pltpu.roll(block, 64, 1)
            return block
        return jnp.zeros((8, 128), jnp.float32)

    for row_z in range(16):
        for pair in range(8):
            for g in range(8):
                a = source(row_z, 2 * pair, g)
                b = source(row_z, 2 * pair + 1, g)
                half[row_z * 64 + g * 8 : row_z * 64 + g * 8 + 8, pair * 128 : pair * 128 + 128] = (
                    jnp.where(lower_lanes, a, b)
                )
    for i in range(8):
        for j in range(i + 1):
            rows, cols = slice(i * 128, i * 128 + 128), slice(j * 128, j * 128 + 128)
            block = half[rows, cols] + half[cols, rows].T
            half[rows, cols] = block
            if i != j:
                half[cols, rows] = block.T


def sweeps_kernel(where_ref, mine, other, rows_ref, cols_ref, half, far, start, basis):
    z, h, c = where_ref[0], where_ref[1], where_ref[2]

    @pl.when(c == 0)
    def _():
        assemble((mine, other), half, far, start, basis)

    @pl.when(c == 1)
    def _():
        assemble((other, mine), half, far, start, basis)

    def sweep(_, carry):
        image = dot(basis[...], half[...], NN)
        correlation = dot(image, image, NT)
        basis[...] = dot(inverse_lower(correlation), image, NN)
        return carry

    lax.fori_loop(0, ITERS, sweep, 0)
    pick = lax.broadcasted_iota(jnp.int32, (32, 1024), 1) == (
        lax.broadcasted_iota(jnp.int32, (32, 1024), 0) + (z * 2 + h) * 32
    )
    rows_ref[...] = dot(jnp.where(pick, 1.0, 0.0), basis[...], NT)
    cols_ref[...] = basis[pl.ds(pl.multiple_of(z * 8, 8), 8), :]


def core_kernel(cols_ref, every_ref, core_ref):
    core_ref[...] = dot(cols_ref[...], every_ref[...], NN)


def core_rows(cols, every):
    return pl.pallas_call(
        core_kernel,
        out_shape=jax.ShapeDtypeStruct((8, 512), jnp.float32),
        in_specs=[pl.BlockSpec(memory_space=pltpu.VMEM)] * 2,
        out_specs=pl.BlockSpec(memory_space=pltpu.VMEM),
        compiler_params=pltpu.CompilerParams(vmem_limit_bytes=16 * 1024 * 1024),
        name="core_rows",
    )(cols, every)


def sweeps(where, mine, other):
    return pl.pallas_call(
        sweeps_kernel,
        out_shape=(
            jax.ShapeDtypeStruct((32, RX), jnp.float32),
            jax.ShapeDtypeStruct((8, 1024), jnp.float32),
        ),
        in_specs=[
            pl.BlockSpec(memory_space=pltpu.SMEM),
            pl.BlockSpec(memory_space=pltpu.VMEM),
            pl.BlockSpec(memory_space=pltpu.VMEM),
        ],
        out_specs=[pl.BlockSpec(memory_space=pltpu.VMEM)] * 2,
        scratch_shapes=[
            pltpu.VMEM((1024, 1024), jnp.float32),
            pltpu.VMEM((8 * 32, 128), jnp.float32),
            pltpu.VMEM((1024, 128), jnp.float32),
            pltpu.VMEM((128, 1024), jnp.float32),
        ],
        compiler_params=pltpu.CompilerParams(vmem_limit_bytes=32 * 1024 * 1024),
        name="sweeps",
    )(where, mine, other)


def local(flow_field, y_factor, z_factor, v_factor, x_start):
    z = lax.axis_index("z").astype(jnp.int32)
    h = lax.axis_index("h").astype(jnp.int32)
    c = lax.axis_index("c").astype(jnp.int32)
    send = reduced_blocks(
        h.reshape(1), flow_field.reshape(1024, NZ * NV), y_factor, z_factor, v_factor
    )
    got = lax.all_to_all(send.reshape(32, 48, 128), PLANE, 0, 0)
    projected, own = projected_rows(got.reshape(32 * 48, 128))

    def from_z(block, distance):
        return lax.ppermute(block, "z", [(i, (i - distance) % 16) for i in range(16)])

    near = {d: from_z(projected, d) for d in (2, -2, 1, -1)}
    for sign in (1, -1):
        pair = from_z(jnp.concatenate([near[sign], near[2 * sign]], axis=0), 2 * sign)
        near[3 * sign], near[4 * sign] = pair[:64], pair[64:]
    near[0] = projected
    blocks = [near[d] for d in range(-4, 5)]

    own, *_ = lax.optimization_barrier((own, near[4], near[-4]))
    every = lax.all_gather(own, "z").reshape(1024, 512)

    part = lax.all_to_all(strips(z, blocks), PLANE, 0, 0).sum(0)
    gy = (lax.axis_index("y") * 4 + lax.axis_index("l") * 2 + c).astype(jnp.int32)
    start = lax.dynamic_slice_in_dim(x_start, 2 * gy, 2, 0)
    part = jnp.concatenate([part[:9], start, jnp.zeros((5, 128), jnp.float32)], axis=0)
    line = lax.all_to_all(jnp.broadcast_to(part[None], (16, 16, 128)), "z", 0, 0)
    line = jnp.concatenate(
        [line[:, :8].reshape(128, 128), line[:8, 8], line[:, 9:11].reshape(32, 128)], axis=0
    )
    mine = lax.all_to_all(jnp.broadcast_to(line[None], (16, PART, 128)), XY, 0, 0)
    mine = mine.reshape(16 * PART, 128)
    other = lax.ppermute(mine, "c", [(0, 1), (1, 0)])

    x_factor, cols = sweeps(jnp.stack([z, h, c]), mine, other)
    core = core_rows(cols, every)
    core = core.reshape(2, 4, 4, 16, 8).transpose(0, 3, 1, 2, 4).reshape(32, 1, 128)
    core = lax.all_to_all(core, PLANE, 0, 0).reshape(32, 4, 4, 8)
    core = core.transpose(1, 3, 0, 2).reshape(4, 1024)
    return (x_factor, core)


def solution(mesh):
    fine = Mesh(mesh.devices.reshape(16, 2, 4, 2, 2), ("z", "h", "y", "l", "c"))
    gx, gy = ("z", "h"), ("y", "l", "c")
    placed = (P(gx, gy, None), P(gy, None), P(), P(), P(gx, None))
    return jax.shard_map(
        local, mesh=fine, in_specs=placed, out_specs=(P(gx, None), P(gx, gy)), check_vma=False
    )
```

```python
import jax
import jax.numpy as jnp
from jax import lax
from jax.experimental import pallas as pl
from jax.experimental.pallas import tpu as pltpu
from jax.sharding import Mesh, PartitionSpec as P

NZ = 64
NV = 32
RX = 128
RY = 128
RZ = 16
RV = 8
ITERS = 3
HIGHEST = lax.Precision.HIGHEST
PLANE = ("h", "y", "l", "c")
XY = ("h", "y", "l")
PART = 168
NN = (((1,), (0,)), ((), ()))
NT = (((1,), (1,)), ((), ()))
TN = (((0,), (0,)), ((), ()))
BLOCKS = 4


def dot(a, b, dims):
    return lax.dot_general(a, b, dims, precision=HIGHEST, preferred_element_type=jnp.float32)


def reduced_kernel(where_ref, flow, small_ref, out_ref, held, table, turned, sems):
    size = 1024 // BLOCKS

    def fetch(j):
        return pltpu.make_async_copy(flow.at[pl.ds(size * j, size), :], held.at[j], sems.at[j])

    for j in range(BLOCKS):
        fetch(j).start()
    wide = lax.broadcasted_iota(jnp.int32, (16, 128), 1) // RV == lax.broadcasted_iota(jnp.int32, (16, 128), 0)
    z_wide = lax.dot_general(
        small_ref[32:48, :], wide.astype(jnp.bfloat16), TN, preferred_element_type=jnp.float32
    )
    wide = lax.broadcasted_iota(jnp.int32, (16, 128), 1) % RV == lax.broadcasted_iota(jnp.int32, (16, 128), 0)
    v_wide = lax.dot_general(
        small_ref[48:64, :], wide.astype(jnp.bfloat16), TN, preferred_element_type=jnp.float32
    )[:NV, :]
    for i in range(NZ):
        table[NV * i : NV * i + NV, :] = (z_wide[i : i + 1, :] * v_wide).astype(jnp.bfloat16)
    half = small_ref[pl.ds(pl.multiple_of(where_ref[0] * 16, 16), 16), :].astype(jnp.float32)
    for p in range(32):
        out_ref[p * 48 + 32 : p * 48 + 48, :] = half
    for i in range(BLOCKS):
        fetch(i).wait()
        block = lax.dot_general(held[i], table[...], NN, preferred_element_type=jnp.float32)
        for part in range(size // 128):
            j = i * (size // 128) + part
            turned[...] = block[part * 128 : part * 128 + 128, :].T.astype(jnp.bfloat16).astype(jnp.float32)
            for k in range(4):
                out_ref[pl.ds(k * 8 + j, 32, stride=48), :] = turned[pl.ds(k, 32, stride=4), :]


def reduced_blocks(where, flow, y_factor, z_factor, v_factor):
    small = jnp.concatenate(
        [
            y_factor,
            jnp.pad(z_factor.T, ((0, 0), (0, 128 - NZ))),
            jnp.pad(v_factor.T, ((0, 16 - RV), (0, 128 - NV))),
        ],
        axis=0,
    )
    return pl.pallas_call(
        reduced_kernel,
        out_shape=jax.ShapeDtypeStruct((32 * 48, 128), jnp.float32),
        in_specs=[pl.BlockSpec(memory_space=pltpu.SMEM), pl.BlockSpec(memory_space=pl.ANY)]
        + [pl.BlockSpec(memory_space=pltpu.VMEM)],
        out_specs=pl.BlockSpec(memory_space=pltpu.VMEM),
        scratch_shapes=[
            pltpu.VMEM((BLOCKS, 1024 // BLOCKS, NZ * NV), jnp.bfloat16),
            pltpu.VMEM((NZ * NV, 128), jnp.bfloat16),
            pltpu.VMEM((128, 128), jnp.float32),
            pltpu.SemaphoreType.DMA((BLOCKS,)),
        ],
        compiler_params=pltpu.CompilerParams(vmem_limit_bytes=53 * 1024 * 1024),
        name="reduced_blocks",
    )(where, flow, small)


def projected_kernel(got, out_ref, own_ref, ordered):
    quarter = lax.broadcasted_iota(jnp.int32, (64, 128), 1) // 32
    total = jnp.zeros((256, 128), jnp.float32)
    for gy in range(0, 16, 2):
        rows, table = [], []
        for g in (gy, gy + 1):
            low, high = g * 48, (16 + g) * 48
            block = jnp.concatenate([got[low : low + 32, :], got[high : high + 32, :]], axis=0)
            rows.append(
                jnp.concatenate([jnp.where(quarter == a, block, 0.0) for a in range(4)], axis=0)
            )
            factor = jnp.concatenate([got[low + 32 : low + 48, :], got[high + 32 : high + 48, :]], axis=0)
            table += [factor] * 4
        rows = jnp.concatenate(rows, axis=1).astype(jnp.bfloat16)
        table = jnp.concatenate(table, axis=0).astype(jnp.bfloat16)
        total = total + lax.dot_general(rows, table, NN, preferred_element_type=jnp.float32)
    for a in range(4):
        for h in range(2):
            for k in range(4):
                base = a * 64 + h * 32 + k * 8
                ordered[pl.ds(k * 64 + h * 32 + a, 8, stride=4), :] = total[base : base + 8, :]
    for k in range(4):
        out_ref[:, k * 128 : k * 128 + 128] = ordered[k * 64 : k * 64 + 64, :]
        own_ref[:, k * 128 : k * 128 + 128] = ordered[k * 64 : k * 64 + 64, :]


def projected_rows(got):
    return pl.pallas_call(
        projected_kernel,
        out_shape=(jax.ShapeDtypeStruct((64, 512), jnp.float32),) * 2,
        in_specs=[pl.BlockSpec(memory_space=pltpu.VMEM)],
        out_specs=[pl.BlockSpec(memory_space=pltpu.VMEM)] * 2,
        scratch_shapes=[pltpu.VMEM((256, 128), jnp.float32)],
        compiler_params=pltpu.CompilerParams(vmem_limit_bytes=16 * 1024 * 1024),
        name="projected_rows",
    )(got)


def strips_kernel(where_ref, *refs):
    blocks, out_ref = refs[:9], refs[9]
    odd = lax.rem(where_ref[0], 2)
    for t in range(4):
        near = blocks[4 + t][...]
        if t == 0:
            near = near * 0.5
        far = blocks[5 + t][...]
        swap = odd != (t % 2)
        pair = jnp.concatenate([jnp.where(swap, far, near), jnp.where(swap, near, far)], axis=0)
        tile = dot(blocks[4 - t][...], pair, NT)
        for g in range(8):
            out_ref[t * 8 + g, 0:8, :] = tile[8 * g : 8 * g + 8, :]
    last = dot(blocks[0][...], blocks[8][...], NT)
    last = jnp.concatenate([last[:32, :], last[32:, :]], axis=1)
    for p in range(32):
        out_ref[p, 8:16, :] = jnp.broadcast_to(last[p : p + 1, :], (8, 128))


def strips(z, blocks):
    return pl.pallas_call(
        strips_kernel,
        out_shape=jax.ShapeDtypeStruct((32, 16, 128), jnp.float32),
        in_specs=[pl.BlockSpec(memory_space=pltpu.SMEM)]
        + [pl.BlockSpec(memory_space=pltpu.VMEM)] * 9,
        out_specs=pl.BlockSpec(memory_space=pltpu.VMEM),
        compiler_params=pltpu.CompilerParams(vmem_limit_bytes=16 * 1024 * 1024),
        name="strips",
    )(z.reshape(1), *blocks)


def inverse_lower(correlation):
    full = (8, 128)
    sub = lax.broadcasted_iota(jnp.int32, full, 0)
    lane = lax.broadcasted_iota(jnp.int32, full, 1)
    left = [correlation[8 * v : 8 * v + 8, :] for v in range(16)]
    right = [jnp.where(lane == sub + 8 * v, 1.0, 0.0) for v in range(16)]
    done = []

    def row(x, i):
        return jnp.broadcast_to(x[i : i + 1, :], full)

    def column(x, j):
        return jnp.broadcast_to(x[:, j : j + 1], full)

    for v in range(16):
        small = [column(left[v], 8 * v + i) for i in range(8)]
        rest, made = left[v], right[v]
        finished = jnp.zeros(full, jnp.float32)
        for i in range(8):
            pivot = row(small[i], i)
            inverse = 1.0 / pivot
            here = sub == i
            share = jnp.where(here, -inverse, small[i] * inverse)
            made_row = row(made, i)
            root = lax.rsqrt(pivot)
            root = root * (1.5 - 0.5 * pivot * root * root)
            finished = jnp.where(here, made_row * root, finished)
            made = jnp.where(here, 0.0, made) - share * made_row
            if v < 15:
                rest = jnp.where(here, 0.0, rest) - share * row(rest, i)
            for k in range(i + 1, 8):
                small[k] = jnp.where(here, 0.0, small[k]) - share * row(small[k], i)
        done.append(finished)
        if v < 15:
            rest_rows = [row(rest, i) for i in range(8)]
            made_rows = [row(made, i) for i in range(8)]
            for w in range(v + 1, 16):
                shares = [column(left[w], 8 * v + i) for i in range(8)]
                taken = [shares[i] * rest_rows[i] for i in range(8)]
                left[w] = left[w] - (
                    ((taken[0] + taken[1]) + (taken[2] + taken[3]))
                    + ((taken[4] + taken[5]) + (taken[6] + taken[7]))
                )
                taken = [shares[i] * made_rows[i] for i in range(8)]
                right[w] = right[w] - (
                    ((taken[0] + taken[1]) + (taken[2] + taken[3]))
                    + ((taken[4] + taken[5]) + (taken[6] + taken[7]))
                )
    return jnp.concatenate(done, axis=0)


def assemble(parts, half, far, start, basis):
    lower_lanes = lax.broadcasted_iota(jnp.int32, (8, 128), 1) < 64

    for zz in range(16):
        for hh in range(2):
            for cc in range(2):
                for e in range(2):
                    start[pl.ds(zz * 64 + hh * 32 + 2 * cc + e, 8, stride=4), :] = parts[cc][
                        pl.ds(hh * 8 * PART + 136 + 2 * zz + e, 8, stride=PART), :
                    ]
    for zz in range(16):
        basis[:, zz * 64 : zz * 64 + 64] = start[zz * 64 : zz * 64 + 64, :].T

    for zz in range(8):
        for cc in range(2):
            for g in range(2):
                far[pl.ds(zz * 32 + cc + 16 * g, 8, stride=2), :] = parts[cc][
                    pl.ds(g * 8 * PART + 128 + zz, 8, stride=PART), :
                ]

    def source(row_z, col_z, g):
        d = (col_z - row_z) % 16
        z_of = (row_z + d // 2) % 16
        if d < 8:
            p = (d // 2) * 8 + g
            base = (p // 2) * PART + z_of * 8
            return parts[p % 2][base : base + 8, :]
        if d == 8 and z_of < 8:
            block = far[z_of * 32 + (g % 4) * 8 : z_of * 32 + (g % 4) * 8 + 8, :]
            if (g >= 4) != (col_z % 2 == 1):
                block = pltpu.roll(block, 64, 1)
            return block
        return jnp.zeros((8, 128), jnp.float32)

    for row_z in range(16):
        for pair in range(8):
            for g in range(8):
                a = source(row_z, 2 * pair, g)
                b = source(row_z, 2 * pair + 1, g)
                half[row_z * 64 + g * 8 : row_z * 64 + g * 8 + 8, pair * 128 : pair * 128 + 128] = (
                    jnp.where(lower_lanes, a, b)
                )
    for i in range(8):
        for j in range(i + 1):
            rows, cols = slice(i * 128, i * 128 + 128), slice(j * 128, j * 128 + 128)
            block = half[rows, cols] + half[cols, rows].T
            half[rows, cols] = block
            if i != j:
                half[cols, rows] = block.T


def sweeps_kernel(where_ref, mine, other, rows_ref, cols_ref, half, far, start, basis):
    z, h, c = where_ref[0], where_ref[1], where_ref[2]

    @pl.when(c == 0)
    def _():
        assemble((mine, other), half, far, start, basis)

    @pl.when(c == 1)
    def _():
        assemble((other, mine), half, far, start, basis)

    def sweep(_, carry):
        image = dot(basis[...], half[...], NN)
        correlation = dot(image, image, NT)
        basis[...] = dot(inverse_lower(correlation), image, NN)
        return carry

    lax.fori_loop(0, ITERS, sweep, 0)
    ahead = pltpu.roll(basis[...], lax.rem((32 - (z * 2 + h)) * 32, 1024), 1)
    rows_ref[...] = ahead[:, :128].T[:32, :]
    cols_ref[...] = basis[pl.ds(pl.multiple_of(z * 8, 8), 8), :]


def sweeps(where, mine, other):
    return pl.pallas_call(
        sweeps_kernel,
        out_shape=(
            jax.ShapeDtypeStruct((32, RX), jnp.float32),
            jax.ShapeDtypeStruct((8, 1024), jnp.float32),
        ),
        in_specs=[
            pl.BlockSpec(memory_space=pltpu.SMEM),
            pl.BlockSpec(memory_space=pltpu.VMEM),
            pl.BlockSpec(memory_space=pltpu.VMEM),
        ],
        out_specs=[pl.BlockSpec(memory_space=pltpu.VMEM)] * 2,
        scratch_shapes=[
            pltpu.VMEM((1024, 1024), jnp.float32),
            pltpu.VMEM((8 * 32, 128), jnp.float32),
            pltpu.VMEM((1024, 128), jnp.float32),
            pltpu.VMEM((128, 1024), jnp.float32),
        ],
        compiler_params=pltpu.CompilerParams(vmem_limit_bytes=32 * 1024 * 1024),
        name="sweeps",
    )(where, mine, other)


def local(flow_field, y_factor, z_factor, v_factor, x_start):
    z = lax.axis_index("z").astype(jnp.int32)
    h = lax.axis_index("h").astype(jnp.int32)
    c = lax.axis_index("c").astype(jnp.int32)
    send = reduced_blocks(
        h.reshape(1), flow_field.reshape(1024, NZ * NV), y_factor, z_factor, v_factor
    )
    got = lax.all_to_all(send.reshape(32, 48, 128), PLANE, 0, 0)
    projected, own = projected_rows(got.reshape(32 * 48, 128))

    def from_z(block, distance):
        return lax.ppermute(block, "z", [(i, (i - distance) % 16) for i in range(16)])

    near = {d: from_z(projected, d) for d in (2, -2, 1, -1)}
    for sign in (1, -1):
        pair = from_z(jnp.concatenate([near[sign], near[2 * sign]], axis=0), 2 * sign)
        near[3 * sign], near[4 * sign] = pair[:64], pair[64:]
    near[0] = projected
    blocks = [near[d] for d in range(-4, 5)]

    own, *_ = lax.optimization_barrier((own, near[4], near[-4]))
    every = lax.all_gather(own, "z").reshape(1024, 512)

    part = lax.all_to_all(strips(z, blocks), PLANE, 0, 0).sum(0)
    gy = (lax.axis_index("y") * 4 + lax.axis_index("l") * 2 + c).astype(jnp.int32)
    start = lax.dynamic_slice_in_dim(x_start, 2 * gy, 2, 0)
    part = jnp.concatenate([part[:9], start, jnp.zeros((5, 128), jnp.float32)], axis=0)
    line = lax.all_to_all(jnp.broadcast_to(part[None], (16, 16, 128)), "z", 0, 0)
    line = jnp.concatenate(
        [line[:, :8].reshape(128, 128), line[:8, 8], line[:, 9:11].reshape(32, 128)], axis=0
    )
    mine = lax.all_to_all(jnp.broadcast_to(line[None], (16, PART, 128)), XY, 0, 0)
    mine = mine.reshape(16 * PART, 128)
    other = lax.ppermute(mine, "c", [(0, 1), (1, 0)])

    x_factor, cols = sweeps(jnp.stack([z, h, c]), mine, other)
    core = dot(cols, every, NN)
    core = core.reshape(2, 4, 4, 16, 8).transpose(0, 3, 1, 2, 4).reshape(32, 1, 128)
    core = lax.all_to_all(core, PLANE, 0, 0).reshape(32, 4, 4, 8)
    core = core.transpose(1, 3, 0, 2).reshape(4, 1024)
    return (x_factor, core)


def solution(mesh):
    fine = Mesh(mesh.devices.reshape(16, 2, 4, 2, 2), ("z", "h", "y", "l", "c"))
    gx, gy = ("z", "h"), ("y", "l", "c")
    placed = (P(gx, gy, None), P(gy, None), P(), P(), P(gx, None))
    return jax.shard_map(
        local, mesh=fine, in_specs=placed, out_specs=(P(gx, None), P(gx, gy)), check_vma=False
    )
```
